256 devices in a mesh: dp: 16 (over x, z_hi), branch: 4 (over z_lo, core), seq: 4 (over y).
Axes of the slice: x: 4, y: 4, z: 8 (z_hi: 4, z_lo: 2; z = z_hi * 2 + z_lo), core: 2. Of those that a mesh axis runs over, the one named last changes fastest.
Arguments:
- qkv: bfloat16 [4, 16, 896, 3, 1536], P('branch', 'dp', 'seq'), may hold values from -5.5 to 5.5, as said below
- grad_base: bfloat16 [16, 896, 2432], P('dp', ('branch', 'seq')), may hold values from -12 to 12
- w_out: bfloat16 [4, 1536, 2432], P('branch', 'seq'), may hold values from -0.15625 to 0.15625
- scale_level: int32 [16], P('dp'), may hold values from 0 to 7
- text_count: int32 [16], P('dp'), may hold values from 96 to 384, as said below
Outputs:
- qkv_grad: bfloat16 [4, 16, 896, 3, 1536], P('branch', 'dp', 'seq')
- w_out_grad: float32 [4, 2432, 1536], P('branch', 'dp', 'seq')
The draws below stay inside these ranges and needn't reach their ends.
Inputs may be any that keep to these rules, and one draw needn't show every extreme that they name: `qkv`: the queries, keys and values are real numbers of order one. `text_count`: some sample has all 384 text slots live in every draw.
All inputs are finite; a program needn't handle non-finite values.
Results may differ from the reference program's by a relative error of at most 0.0064.
Values may be sent and summed in bfloat16 or wider, within the bound.
No kernel may reach another device: no remote copies, remote signals or barrier semaphores. Data moves between devices by JAX's collectives and lax.ppermute only.
A program may use at most 64 MiB of HBM per device.

```python
import math
import jax
import jax.numpy as jnp
from jax import lax

D = 2432
DH = 64
LAT = 512
TXT = 384
SCALE_LEVELS = 8
SEQ = 896
HD = 1536
GROUPS = 4
BATCH = 16


def draw_qkv(key, part):
    key = jax.random.fold_in(key, 11)
    key_base = jax.random.fold_in(key, 0)
    full_shape = (GROUPS, BATCH, SEQ, 3, HD)
    values = jnp.clip(jax.random.normal(key_base, full_shape, jnp.float32), -4.5, 4.5)
    return values.astype(jnp.bfloat16)


def draw_text_count(key, part):
    key = jax.random.fold_in(key, 23)
    key_counts, key_chosen = jax.random.split(key, 2)
    counts = jax.random.randint(key_counts, (BATCH,), TXT // 4, TXT + 1)
    chosen = jax.random.randint(key_chosen, (), 0, BATCH)
    return jnp.where(jnp.arange(BATCH) == chosen, TXT, counts).astype(jnp.int32)


def set_ends(values, key, low, high):
    index_at = [jax.random.randint(jax.random.fold_in(key, axis), (), 0, length) for axis, length in enumerate(values.shape)]
    main_axis = values.shape.index(max(values.shape))
    neighbour = index_at[:main_axis] + [(index_at[main_axis] + 1) % values.shape[main_axis]] + index_at[main_axis + 1:]
    return values.at[tuple(index_at)].set(low).at[tuple(neighbour)].set(high)


def with_spikes(array, own_key, source, target, blocks, factor):
    def block_of(dim):
        return (jnp.arange(array.shape[dim]) // (array.shape[dim] // blocks)).reshape((-1,) + (1,) * (array.ndim - 1 - dim))

    first = jax.random.permutation(own_key, blocks)[block_of(target)]
    second = (block_of(target) + blocks // 2) % blocks
    return jnp.where((block_of(source) == first) | (block_of(source) == second), factor * array, array)


def block_levels(own_key, dims, cuts, least, largest):
    level = 1.0
    for axis_at, blocks in cuts:
        draws = jax.random.uniform(jax.random.fold_in(jax.random.fold_in(own_key, 6), axis_at), (blocks,), jnp.float32, least / len(cuts), largest / len(cuts))
        level = level * jnp.repeat(jnp.exp(draws), dims[axis_at] // blocks).reshape((-1,) + (1,) * (len(dims) - 1 - axis_at))
    return level


def noise(own_key, dims, width, most, shards=(), dtype=jnp.bfloat16):
    values = jax.random.normal(own_key, dims, jnp.float32) * width
    if len(shards) > 0:
        values = block_levels(own_key, dims, shards, -0.22, 0.18) * values
    return jnp.clip(values, min=-most, max=most).astype(dtype)


def noise_with(key, extent, scale, limit, shards, heavy, dtype=jnp.bfloat16):
    values = scale * jax.random.normal(key, extent, jnp.float32)
    if shards:
        values = values * block_levels(key, extent, shards, -0.22, 0.18)
    return jnp.clip(with_spikes(values, jax.random.fold_in(key, 3), *heavy), -limit, limit).astype(dtype)


def setup_inputs(seed: int = 0) -> dict:
    streams_of = jax.random.split(jax.random.key(seed), 6)
    qkv = draw_qkv(jax.random.fold_in(streams_of[5], 71), 0)
    grad_base = noise_with(streams_of[1], (BATCH, SEQ, D), 2.0, 12.0, ((0, 16), (1, 16)), (0, 2, 16, 2.0))
    w_out = noise(streams_of[2], (GROUPS, HD, D), HD ** -0.5, 0.15625, ((0, 4), (1, 4)))
    scale_level = set_ends(jax.random.randint(streams_of[3], (BATCH,), 0, SCALE_LEVELS), jax.random.fold_in(streams_of[3], 1), 0, SCALE_LEVELS - 1).astype(jnp.int32)
    text_count = draw_text_count(jax.random.fold_in(streams_of[5], 71), 0)
    return dict(qkv=qkv, grad_base=grad_base, w_out=w_out, scale_level=scale_level, text_count=text_count)


def head_grads(queries, keys_h, values_h, out_grad, key_valid):
    inv_root = 1.0 / math.sqrt(queries.shape[-1])
    scores = jnp.dot(queries, keys_h.T, preferred_element_type=jnp.float32) * inv_root
    scores = jnp.where(key_valid[None, :], scores, -jnp.inf)
    row_max = lax.optimization_barrier(jnp.max(scores, axis=1, keepdims=True))
    powers = jnp.exp(scores - row_max)
    probs = powers / lax.optimization_barrier(jnp.sum(powers, axis=1, keepdims=True))
    probs_b = probs.astype(jnp.bfloat16)
    attended = jnp.dot(probs_b, values_h, preferred_element_type=jnp.float32).astype(jnp.bfloat16)
    prob_grad = jnp.dot(out_grad, values_h.T, preferred_element_type=jnp.float32)
    row_dot = lax.optimization_barrier(jnp.sum(probs * prob_grad, axis=1, keepdims=True))
    score_grad = (probs * (prob_grad - row_dot)).astype(jnp.bfloat16)
    query_grad = jnp.dot(score_grad, keys_h, preferred_element_type=jnp.float32) * inv_root
    key_grad = jnp.dot(score_grad.T, queries, preferred_element_type=jnp.float32) * inv_root
    value_grad = jnp.dot(probs_b.T, out_grad, preferred_element_type=jnp.float32)
    return (attended, query_grad, key_grad, value_grad)

def attend(activation, upstream, weight, factor, key_valid):
    token_count = activation.shape[0]
    feature_width = weight.shape[0]
    head_count = feature_width // DH
    out_grad = (jnp.dot(upstream, weight.T, preferred_element_type=jnp.float32) * factor).astype(jnp.bfloat16)

    def split_heads(matrix):
        return matrix.reshape(token_count, head_count, DH).transpose(1, 0, 2)

    def join_heads(matrix):
        return matrix.transpose(1, 0, 2).reshape(token_count, feature_width)

    def one_head(pieces):
        return head_grads(pieces[0], pieces[1], pieces[2], pieces[3], key_valid)
    attended, query_grad, key_grad, value_grad = lax.map(one_head, (split_heads(activation[:, 0]), split_heads(activation[:, 1]), split_heads(activation[:, 2]), split_heads(out_grad)))
    act_grads = jnp.stack([join_heads(query_grad), join_heads(key_grad), join_heads(value_grad)], axis=1).astype(jnp.bfloat16)
    return (act_grads, join_heads(attended))

def reference(qkv, grad_base, w_out, scale_level, text_count):
    levels = jnp.arange(SCALE_LEVELS)
    groups = jnp.arange(GROUPS)
    scale_table = jnp.where(groups[None, :] == 0, jnp.float32(1.0), (levels[:, None] + 2 * groups[None, :]).astype(jnp.float32) / 8.0).astype(jnp.float32)
    factors = scale_table[scale_level]
    positions = jnp.arange(SEQ)

    def per_group(pieces):
        group_acts, weight, column = pieces

        def per_sample(running, sample):
            activation, upstream, factor, live_count = sample
            key_valid = positions < LAT + live_count
            act_grads, attended = attend(activation, upstream, weight, factor, key_valid)
            term = jnp.dot(upstream.T, attended, preferred_element_type=jnp.float32) * factor
            return (running + term, act_grads)
        running, act_grads = lax.scan(per_sample, jnp.zeros((D, HD), jnp.float32), (group_acts, grad_base, column, text_count))
        return (act_grads, running)
    qkv_grad, w_out_grad = lax.map(per_group, (qkv, w_out, factors.T))
    return (qkv_grad, w_out_grad)
```

```python
import math

import jax
import jax.numpy as jnp
from jax import lax
from jax.experimental import pallas as pl
from jax.experimental.pallas import tpu as pltpu
from jax.sharding import PartitionSpec as P

LAT = 512
LIVE = 608
SEQ = 896
TOK = 224
PAIR = 128
CHUNKS = 3
D = 2432
HDL = 384
RX = 608
RZ = 152
EXP_SCALE = math.log2(math.e) / 8.0
NN = (((1,), (0,)), ((), ()))
NT = (((1,), (1,)), ((), ()))
BF = jnp.bfloat16
F32 = jnp.float32

VMEM = pl.BlockSpec(memory_space=pltpu.VMEM)
SMEM = pl.BlockSpec(memory_space=pltpu.SMEM)
HBM = pl.BlockSpec(memory_space=pl.ANY)


def dot(a, b, dims=NN):
    return lax.dot_general(a, b, dims, preferred_element_type=F32)


def sds(shape, dtype=BF):
    return jax.ShapeDtypeStruct(shape, dtype)


def params(mib=40):
    return pltpu.CompilerParams(vmem_limit_bytes=mib << 20)


def cost(flops, nbytes):
    return pl.CostEstimate(flops=int(flops), bytes_accessed=int(nbytes), transcendentals=0)


def row(index, size):
    return pl.ds(pl.multiple_of(index * size, size), size)


def factor_of(info):
    value = (info[3] + 2 * info[1]).astype(F32) * 0.125
    return jnp.where(info[1] == 0, jnp.float32(1.0), value)


def assemble_kernel(info, g0, g1, g2, g3, out, sems):
    copies = []
    for s, ref in enumerate((g0, g1, g2, g3)):
        dst = out.at[lax.rem(info[0] + 4 - s, 4)]
        copies.append(pltpu.make_async_copy(ref, dst, sems.at[s]))
    for copy in copies:
        copy.start()
    for copy in copies:
        copy.wait()


def assemble(info, parts):
    return pl.pallas_call(
        assemble_kernel,
        in_specs=[SMEM] + [HBM] * 4,
        out_specs=HBM,
        out_shape=sds((4, 56, D)),
        scratch_shapes=[pltpu.SemaphoreType.DMA((4,))],
        cost_estimate=cost(0, 4 << 20),
        name="assemble",
    )(info, *parts)


def forward_kernel(info, x0, x1, x2, x3, att, probs, k_ref, q, k, v):
    me = info[0]
    limit = info[2]
    for s, ref in enumerate((x0, x1, x2, x3)):
        at = row(lax.rem(me + 4 - s, 4), TOK)
        q[at, :] = ref[0]
        k[at, :] = ref[1]
        v[at, :] = ref[2]
    k_ref[0] = q[...]
    k_ref[1] = k[...]
    k_ref[2] = v[...]
    low = lax.broadcasted_iota(jnp.int32, (SEQ, PAIR), 1) < 64
    tail = lax.broadcasted_iota(jnp.int32, (SEQ - LIVE, 1), 0) + LIVE
    keys = k[...]
    queries = q[...]
    values_t = v[...].T
    zero = jnp.zeros_like(keys)
    out = []
    for h in range(2):
        keys_h = jnp.where(low, keys, zero) if h == 0 else jnp.where(low, zero, keys)
        scores = dot(keys_h, queries, NT)
        scores = jnp.concatenate(
            [scores[:LIVE], jnp.where(tail < limit, scores[LIVE:], -jnp.inf)], axis=0
        )
        top = jnp.max(scores, axis=0, keepdims=True)
        powers = jnp.exp2((scores - top) * EXP_SCALE)
        total = jnp.sum(powers, axis=0, keepdims=True)
        probs_b = (powers * (1.0 / total)).astype(BF)
        probs[h] = probs_b
        out.append(dot(values_t[h * 64 : (h + 1) * 64], probs_b))
    att[...] = jnp.concatenate(out, axis=0).T


def forward(info, parts):
    return pl.pallas_call(
        forward_kernel,
        in_specs=[SMEM] + [VMEM] * 4,
        out_specs=[VMEM] * 3,
        out_shape=[sds((SEQ, PAIR), F32), sds((2, SEQ, SEQ)), sds((3, SEQ, PAIR))],
        scratch_shapes=[pltpu.VMEM((SEQ, PAIR), BF)] * 3,
        compiler_params=params(),
        cost_estimate=cost(4e9, 6 << 20),
        name="forward",
    )(info, *parts)


def project_kernel(info, u0, u1, u2, u3, w, out):
    factor = factor_of(info)
    for r, ref in enumerate((u0, u1, u2, u3)):
        out[row(info[1] ^ r, TOK), :] = (dot(ref[...], w[...], NT) * factor).astype(BF)


def project(info, ups, weight):
    return pl.pallas_call(
        project_kernel,
        in_specs=[SMEM] + [VMEM] * 5,
        out_specs=VMEM,
        out_shape=sds((SEQ, HDL)),
        compiler_params=params(),
        cost_estimate=cost(2 * SEQ * D * HDL, 8 << 20),
        name="project",
    )(info, *ups, weight)


def weight_kernel(info, xi, u0, u1, u2, u3, a0, a1, a2, o0, o1, o2, o3, up, att_t, total, sems):
    copies = []
    for r, ref in enumerate((u0, u1, u2, u3)):
        copies.append(pltpu.make_async_copy(ref, up.at[row(info[1] ^ r, TOK), :], sems.at[r]))
    for copy in copies:
        copy.start()
    for c, ref in enumerate((a0, a1, a2)):
        att_t[c * PAIR : (c + 1) * PAIR, :] = ref[...].astype(BF).T
    factor = factor_of(info)
    for copy in copies:
        copy.wait()
    for at in range(0, D, 256):
        size = min(256, D - at)
        term = dot(att_t[...], up[:, at : at + size]) * factor
        total[at : at + size, :] = term.T.astype(BF)
    for s, ref in enumerate((o0, o1, o2, o3)):
        ref[...] = total[row(lax.rem(xi[0] + s, 4), RX), :]


def weight_terms(info, xi, ups, atts):
    return pl.pallas_call(
        weight_kernel,
        in_specs=[SMEM] * 2 + [HBM] * 4 + [VMEM] * 3,
        out_specs=[VMEM] * 4,
        out_shape=[sds((RX, HDL))] * 4,
        scratch_shapes=[
            pltpu.VMEM((SEQ, D), BF),
            pltpu.VMEM((HDL, SEQ), BF),
            pltpu.VMEM((D, HDL), BF),
            pltpu.SemaphoreType.DMA((4,)),
        ],
        compiler_params=params(),
        cost_estimate=cost(2 * SEQ * D * HDL, 8 << 20),
        name="weight",
    )(info, xi, *ups, *atts)


def first_sum_kernel(xi, p0, p1, p2, p3, own, o1, o2, o3, total):
    total[...] = (p0[...].astype(F32) + p1[...].astype(F32)) + (
        p2[...].astype(F32) + p3[...].astype(F32)
    )
    own[...] = total[row(xi[1], RZ), :]
    for s, ref in enumerate((o1, o2, o3)):
        ref[...] = total[row(lax.rem(xi[1] + s + 1, 4), RZ), :].astype(BF)


def first_sum(xi, parts):
    return pl.pallas_call(
        first_sum_kernel,
        in_specs=[SMEM] + [VMEM] * 4,
        out_specs=[VMEM] * 4,
        out_shape=[sds((RZ, HDL), F32)] + [sds((RZ, HDL))] * 3,
        scratch_shapes=[pltpu.VMEM((RX, HDL), F32)],
        compiler_params=params(),
        cost_estimate=cost(0, 3 << 20),
        name="first_sum",
    )(xi, *parts)


def backward_kernel(info, qkv, do_ref, att, probs, o0, o1, o2, o3, dq, dk, dv):
    low = lax.broadcasted_iota(jnp.int32, (SEQ, PAIR), 1) < 64
    queries, keys, values = qkv[0], qkv[1], qkv[2]
    keys_t = keys.T
    grads = do_ref[...]
    zero = jnp.zeros_like(keys)
    products = (grads.astype(F32) * att[...]).T
    query_t = []
    key_sum = 0.0
    value_sum = 0.0
    for h in range(2):
        pick = (lambda a: jnp.where(low, a, zero)) if h == 0 else (lambda a: jnp.where(low, zero, a))
        row_dot = jnp.sum(products[h * 64 : (h + 1) * 64], axis=0, keepdims=True)
        prob_grad = dot(pick(values), grads, NT)
        score_grad = (probs[h].astype(F32) * (prob_grad - row_dot)).astype(BF)
        query_t.append(dot(keys_t[h * 64 : (h + 1) * 64], score_grad))
        key_sum = key_sum + dot(score_grad, pick(queries))
        value_sum = value_sum + dot(probs[h], pick(grads))
    dq[...] = (jnp.concatenate(query_t, axis=0) * 0.125).T.astype(BF)
    dk[...] = (key_sum * 0.125).astype(BF)
    dv[...] = value_sum.astype(BF)
    for s, ref in enumerate((o0, o1, o2, o3)):
        at = row(lax.rem(info[0] + s, 4), TOK)
        ref[0] = dq[at, :]
        ref[1] = dk[at, :]
        ref[2] = dv[at, :]


def backward(info, chunk, qkv, out_grad, att, probs):
    return pl.pallas_call(
        backward_kernel,
        grid=(1,),
        in_specs=[
            SMEM,
            VMEM,
            pl.BlockSpec((SEQ, PAIR), lambda i: (0, chunk)),
            VMEM,
            VMEM,
        ],
        out_specs=[VMEM] * 4,
        out_shape=[sds((3, TOK, PAIR))] * 4,
        scratch_shapes=[pltpu.VMEM((SEQ, PAIR), BF)] * 3,
        compiler_params=params(),
        cost_estimate=cost(5e9, 6 << 20),
        name="backward",
    )(info, qkv, out_grad, att, probs)


def place_kernel(info, *refs):
    parts, out, sems = refs[:12], refs[12], refs[13]
    copies = []
    for n, ref in enumerate(parts):
        c, s = divmod(n, 4)
        source = lax.rem(info[0] + 4 - s, 4)
        at = pl.multiple_of(source * HDL + c * PAIR, PAIR)
        copies.append(pltpu.make_async_copy(ref, out.at[:, :, pl.ds(at, PAIR)], sems.at[n]))
    for copy in copies:
        copy.start()
    for copy in copies:
        copy.wait()


def place(info, parts):
    return pl.pallas_call(
        place_kernel,
        in_specs=[SMEM] + [HBM] * 12,
        out_specs=HBM,
        out_shape=sds((3, TOK, 4 * HDL)),
        scratch_shapes=[pltpu.SemaphoreType.DMA((12,))],
        cost_estimate=cost(0, 4 << 20),
        name="place",
    )(info, *parts)


def rotate(x, s):
    return lax.ppermute(x, "seq", [(i, (i + s) % 4) for i in range(4)])


def rotate_x(x, s):
    return lax.ppermute(x, "dp", [(i, (i + 4 * s) % 16) for i in range(16)])


def rotate_z(x, s):
    return lax.ppermute(x, "dp", [(i, i - i % 4 + (i + s) % 4) for i in range(16)])


def across(x, bit):
    return lax.ppermute(x, "branch", [(i, i ^ bit) for i in range(4)])


def body(qkv, grad_base, w_out, scale_level, text_count):
    me = lax.axis_index("seq")
    branch = lax.axis_index("branch")
    dp = lax.axis_index("dp")
    info = jnp.stack([me, branch, LAT + text_count[0], scale_level[0]]).astype(jnp.int32)
    xi = jnp.stack([dp // 4, dp % 4]).astype(jnp.int32)

    rows = grad_base[0]
    near = [rows] + [rotate(rows, s) for s in (1, 2, 3)]
    own = assemble(info, near).reshape(TOK, D)
    beside = across(own, 1)
    far = across(own, 2)
    corner = across(far, 1)
    ups = [own, beside, far, corner]

    tokens = qkv[0, 0].transpose(1, 0, 2)

    def cut(c, s):
        at = lax.rem(me + s, 4) * HDL + c * PAIR
        return lax.dynamic_slice(tokens, (0, 0, at), (3, TOK, PAIR))

    states = []
    for c in range(CHUNKS):
        parts = [cut(c, 0)] + [rotate(cut(c, s), s) for s in (1, 2, 3)]
        states.append(forward(info, parts))
    out_grad = project(info, ups, w_out[0])
    terms = weight_terms(info, xi, ups, [state[0] for state in states])
    sums = first_sum(xi, [terms[0]] + [rotate_x(terms[s], s) for s in (1, 2, 3)])
    final = sums[0]
    for s in (1, 2, 3):
        final = final + rotate_z(sums[s], s).astype(F32)

    pieces = []
    for c in range(CHUNKS):
        att, probs, heads = states[c]
        back = backward(info, c, heads, out_grad, att, probs)
        pieces += [back[0]] + [rotate(back[s], s) for s in (1, 2, 3)]
    grads = place(info, pieces)
    return grads.transpose(1, 0, 2)[None, None], final[None]


def solution(mesh):
    in_specs = (
        P("branch", "dp", "seq", None, None),
        P("dp", ("branch", "seq"), None),
        P("branch", "seq", None),
        P("dp"),
        P("dp"),
    )
    out_specs = (P("branch", "dp", "seq", None, None), P("branch", "dp", "seq"))
    return jax.shard_map(body, mesh=mesh, in_specs=in_specs, out_specs=out_specs, check_vma=False)
```

```python
import functools
import math

import jax
import jax.numpy as jnp
from jax import lax
from jax.experimental import pallas as pl
from jax.experimental.pallas import tpu as pltpu
from jax.sharding import Mesh
from jax.sharding import PartitionSpec as P

LAT = 512
LIVE = 608
SEQ = 896
TOK = 224
PAIR = 128
D = 2432
HDL = 384
RX = 608
RZ = 152
EXP_SCALE = math.log2(math.e) / 8.0
NN = (((1,), (0,)), ((), ()))
NT = (((1,), (1,)), ((), ()))
BF = jnp.bfloat16
F32 = jnp.float32

VMEM = pl.BlockSpec(memory_space=pltpu.VMEM)
SMEM = pl.BlockSpec(memory_space=pltpu.SMEM)
AUTO = pl.BlockSpec()
HBM = pl.BlockSpec(memory_space=pl.ANY)


def dot(a, b, dims=NN):
    return lax.dot_general(a, b, dims, preferred_element_type=F32)


def sds(shape, dtype=BF):
    return jax.ShapeDtypeStruct(shape, dtype)


def params(mib=32):
    return pltpu.CompilerParams(vmem_limit_bytes=mib << 20)


def cost(flops, nbytes):
    return pl.CostEstimate(flops=0, bytes_accessed=0, transcendentals=0)


def row(index, size):
    return pl.ds(pl.multiple_of(index * size, size), size)


def factor_of(info):
    value = (info[3] + 2 * info[1]).astype(F32) * 0.125
    return jnp.where(info[1] == 0, jnp.float32(1.0), value)


def stack_kernel(g1, g2, g3, first, rest):
    for s, ref in enumerate((g1, g2, g3)):
        rest[s] = ref[...]


def stack_rows(parts):
    return pl.pallas_call(
        stack_kernel,
        in_specs=[VMEM] * 3 + [HBM],
        out_specs=VMEM,
        out_shape=sds((3, 56, D)),
        compiler_params=params(8),
        cost_estimate=pl.CostEstimate(flops=int(2e+10), bytes_accessed=0, transcendentals=0),
        name="stack_rows",
    )(*parts)


def order_kernel(info, g0, rest, f0, far, out):
    for r, (one, three) in enumerate(((g0, rest), (f0, far))):
        out[4 * r + info[0]] = one[...]
        for s in (1, 2, 3):
            out[4 * r + lax.rem(info[0] + 4 - s, 4)] = three[s - 1]


def order_rows(info, parts):
    return pl.pallas_call(
        order_kernel,
        in_specs=[SMEM] + [VMEM] * 4,
        out_specs=VMEM,
        out_shape=sds((8, 56, D)),
        compiler_params=params(8),
        cost_estimate=cost(0, 2 << 20),
        name="order_rows",
    )(info, *parts)


def cut_kernel(info, tokens, *outs):
    for s in range(4):
        base = lax.rem(info[0] + s, 4) * HDL
        for c in range(3):
            at = pl.ds(pl.multiple_of(base + c * PAIR, PAIR), PAIR)
            if c < 2:
                outs[s][:, :, c * PAIR : (c + 1) * PAIR] = tokens[:, :, at]
            else:
                outs[4 + s][...] = tokens[:, :, at]


def cut_tokens(info, tokens):
    widths = [2 * PAIR] * 4 + [PAIR] * 4
    outs = pl.pallas_call(
        cut_kernel,
        grid=(3,),
        in_specs=[SMEM, pl.BlockSpec((1, TOK, 4 * HDL), lambda i: (i, 0, 0))],
        out_specs=[pl.BlockSpec((1, TOK, w), lambda i: (i, 0, 0)) for w in widths],
        out_shape=[sds((3, TOK, w)) for w in widths],
        compiler_params=params(8),
        cost_estimate=cost(0, 4 << 20),
        name="cut_tokens",
    )(info, tokens)
    return list(outs[:4]), list(outs[4:])


def forward_kernel(info, x0, x1, x2, x3, att, probs, k_ref):
    me = info[0]
    limit = info[2]
    for s, ref in enumerate((x0, x1, x2, x3)):
        at = row(lax.rem(me + 4 - s, 4), TOK)
        for n in range(3):
            k_ref[n, at, :] = ref[n]
    low = lax.broadcasted_iota(jnp.int32, (SEQ, PAIR), 1) < 64
    tail = lax.broadcasted_iota(jnp.int32, (SEQ - LIVE, 1), 0) + LIVE
    for c in range(x0.shape[2] // PAIR):
        lanes = slice(c * PAIR, (c + 1) * PAIR)
        queries = k_ref[0, :, lanes]
        keys = k_ref[1, :, lanes]
        values_t = k_ref[2, :, lanes].T
        zero = jnp.zeros_like(keys)
        out = []
        for h in range(2):
            keys_h = jnp.where(low, keys, zero) if h == 0 else jnp.where(low, zero, keys)
            scores = dot(keys_h, queries, NT)
            scores = jnp.concatenate(
                [scores[:LIVE], jnp.where(tail < limit, scores[LIVE:], -jnp.inf)], axis=0
            )
            top = jnp.max(scores, axis=0, keepdims=True)
            powers = jnp.exp2((scores - top) * EXP_SCALE)
            total = jnp.sum(powers, axis=0, keepdims=True)
            probs_b = (powers * (1.0 / total)).astype(BF)
            probs[2 * c + h] = probs_b
            out.append(dot(values_t[h * 64 : (h + 1) * 64], probs_b))
        att[:, lanes] = jnp.concatenate(out, axis=0).T


def forward(info, parts):
    width = parts[0].shape[2]
    pairs = width // PAIR
    return pl.pallas_call(
        forward_kernel,
        in_specs=[SMEM] + [AUTO] * 4,
        out_specs=[VMEM] * 3,
        out_shape=[sds((SEQ, width), F32), sds((2 * pairs, SEQ, SEQ)), sds((3, SEQ, width))],
        compiler_params=params(),
        cost_estimate=pl.CostEstimate(flops=int(6e+10), bytes_accessed=0, transcendentals=0),
        name="forward",
    )(info, *parts)


def project_kernel(info, u0, u1, w, out):
    factor = factor_of(info)
    for r in range(4):
        ref = (u0, u1)[r % 2]
        part = ref[r // 2 * TOK : (r // 2 + 1) * TOK]
        out[row(info[1] ^ r, TOK), :] = (dot(part, w[...], NT) * factor).astype(BF)


def project(info, ups, weight):
    return pl.pallas_call(
        project_kernel,
        in_specs=[SMEM] + [VMEM] * 3,
        out_specs=VMEM,
        out_shape=sds((SEQ, HDL)),
        compiler_params=params(),
        cost_estimate=cost(2 * SEQ * D * HDL, 8 << 20),
        name="project",
    )(info, *ups, weight)


def weight_kernel(info, u0, u1, a_ref, b_ref, o0, o1, o2, o3, att_t, total):
    for r in range(4):
        at = row(info[1] ^ r, TOK)
        att_t[r, : 2 * PAIR] = a_ref[at, :].astype(BF).T
        att_t[r, 2 * PAIR :] = b_ref[at, :].astype(BF).T
    factor = factor_of(info)
    for at in range(0, D, 256):
        size = min(256, D - at)
        term = 0.0
        for r in range(4):
            part = (u0, u1)[r % 2][r // 2 * TOK : (r // 2 + 1) * TOK, at : at + size]
            term = term + dot(att_t[r], part)
        total[at : at + size, :] = (term * factor).T.astype(BF)
    for s, ref in enumerate((o0, o1, o2, o3)):
        ref[...] = total[row(lax.rem(info[4] + s, 4), RX), :]


def weight_terms(info, ups, atts):
    return pl.pallas_call(
        weight_kernel,
        in_specs=[SMEM] + [VMEM] * 4,
        out_specs=[VMEM] * 4,
        out_shape=[sds((RX, HDL))] * 4,
        scratch_shapes=[pltpu.VMEM((4, HDL, TOK), BF), pltpu.VMEM((D, HDL), BF)],
        compiler_params=params(),
        cost_estimate=cost(2 * SEQ * D * HDL, 8 << 20),
        name="weight",
    )(info, *ups, *atts)


def first_sum_kernel(info, p0, p1, p2, p3, own, o1, o2, o3, total):
    total[...] = (p0[...].astype(F32) + p1[...].astype(F32)) + (
        p2[...].astype(F32) + p3[...].astype(F32)
    )
    for s, ref in enumerate((own, o1, o2, o3)):
        ref[...] = total[row(lax.rem(info[5] + s, 4), RZ), :].astype(ref.dtype)


def first_sum(info, parts):
    return pl.pallas_call(
        first_sum_kernel,
        in_specs=[SMEM] + [VMEM] * 4,
        out_specs=[VMEM] * 4,
        out_shape=[sds((RZ, HDL), F32), sds((RZ, HDL), F32)] + [sds((RZ, HDL))] * 2,
        scratch_shapes=[pltpu.VMEM((RX, HDL), F32)],
        compiler_params=params(8),
        cost_estimate=cost(0, 3 << 20),
        name="first_sum",
    )(info, *parts)


def backward_kernel(info, qkv, do_ref, att, probs, o0, o1, o2, o3, out):
    low = lax.broadcasted_iota(jnp.int32, (SEQ, PAIR), 1) < 64
    for c in range(qkv.shape[2] // PAIR):
        lanes = slice(c * PAIR, (c + 1) * PAIR)
        queries, keys, values = qkv[0, :, lanes], qkv[1, :, lanes], qkv[2, :, lanes]
        keys_t = keys.T
        grads = do_ref[:, lanes]
        zero = jnp.zeros_like(keys)
        products = (grads.astype(F32) * att[:, lanes]).T
        query_t = []
        key_sum = 0.0
        value_sum = 0.0
        for h in range(2):

            def pick(a):
                return jnp.where(low, a, zero) if h == 0 else jnp.where(low, zero, a)

            row_dot = jnp.sum(products[h * 64 : (h + 1) * 64], axis=0, keepdims=True)
            prob_grad = dot(pick(values), grads, NT)
            probs_b = probs[2 * c + h]
            score_grad = (probs_b.astype(F32) * (prob_grad - row_dot)).astype(BF)
            query_t.append(dot(keys_t[h * 64 : (h + 1) * 64], score_grad))
            key_sum = key_sum + dot(score_grad, pick(queries))
            value_sum = value_sum + dot(probs_b, pick(grads))
        out[0, :, lanes] = (jnp.concatenate(query_t, axis=0) * 0.125).T.astype(BF)
        out[1, :, lanes] = (key_sum * 0.125).astype(BF)
        out[2, :, lanes] = value_sum.astype(BF)
    for s, ref in enumerate((o0, o1, o2, o3)):
        at = row(lax.rem(info[0] + s, 4), TOK)
        for n in range(3):
            ref[n] = out[n, at, :]


def backward(info, first, qkv, out_grad, att, probs):
    width = qkv.shape[2]
    return pl.pallas_call(
        backward_kernel,
        grid=(1,),
        in_specs=[
            SMEM,
            VMEM,
            pl.BlockSpec((SEQ, width), lambda i: (0, first * PAIR // width)),
            VMEM,
            VMEM,
        ],
        out_specs=[VMEM] * 4,
        out_shape=[sds((3, TOK, width))] * 4,
        scratch_shapes=[pltpu.VMEM((3, SEQ, width), BF)],
        compiler_params=params(),
        cost_estimate=cost(5e9 * (width // PAIR), 6 << 20),
        name="backward",
    )(info, qkv, out_grad, att, probs)


def place_kernel(info, *refs):
    out = refs[-1]
    for s in range(4):
        source = lax.rem(info[0] + 4 - s, 4)
        for base, ref in ((0, refs[s]), (2 * PAIR, refs[4 + s])):
            for c in range(ref.shape[2] // PAIR):
                at = pl.multiple_of(source * HDL + base + c * PAIR, PAIR)
                for n in range(3):
                    out[n, :, pl.ds(at, PAIR)] = ref[n, :, c * PAIR : (c + 1) * PAIR]


def place(info, parts):
    return pl.pallas_call(
        place_kernel,
        in_specs=[SMEM] + [VMEM] * 8,
        out_specs=VMEM,
        out_shape=sds((3, TOK, 4 * HDL)),
        compiler_params=params(8),
        cost_estimate=cost(0, 4 << 20),
        name="place",
    )(info, *parts)


def rotate(x, s, axis="seq"):
    return lax.ppermute(x, axis, [(i, (i + s) % 4) for i in range(4)])


def across(x, bit):
    return lax.ppermute(x, "branch", [(i, i ^ bit) for i in range(4)])


def after(x, *first):
    return lax.optimization_barrier((x, *first))[0]


def body(qkv, grad_base, w_out, scale_level, text_count):
    me = lax.axis_index("seq")
    branch = lax.axis_index("branch")
    live = LAT + text_count[0]
    info = [me, branch, live, scale_level[0], lax.axis_index("x"), lax.axis_index("zh")]
    info = jnp.stack(info).astype(jnp.int32)

    tokens = qkv[0, 0].transpose(1, 0, 2)
    first, second = cut_tokens(info, tokens)
    rows = grad_base[0]
    near = [rows] + [rotate(rows, s) for s in (1, 2, 3)]
    far_row = across(rows, 2)
    for s in (1, 2, 3):
        first[s] = rotate(after(first[s], near[s]), s)
    rest = stack_rows(near[1:] + [far_row])
    far_rest = across(rest, 2)
    here = order_rows(info, [rows, rest, far_row, far_rest])
    ups = [here, across(here, 1)]
    ups = [part.reshape(2 * TOK, D) for part in ups]
    for s in (1, 2, 3):
        second[s] = rotate(after(second[s], first[s]), s)

    att_a, probs_a, heads_a = forward(info, first)
    second[0] = after(second[0], att_a)
    att_b, probs_b, heads_b = forward(info, second)
    out_grad = project(info, ups, after(w_out[0], att_b))
    terms = weight_terms(info, ups, [att_a, after(att_b, out_grad)])
    sent = [terms[0]] + [rotate(terms[s], s, "x") for s in (1, 2, 3)]
    back_a = backward(info, 0, after(heads_a, terms[0]), out_grad, att_a, probs_a)
    pieces = [back_a[0]] + [rotate(back_a[s], s) for s in (1, 2, 3)]
    back_b = backward(info, 2, after(heads_b, back_a[0]), out_grad, att_b, probs_b)

    sent[0] = after(sent[0], back_b[0])
    sums = first_sum(info, sent)
    step = rotate(sums[2], 1, "zh")
    pieces += [back_b[0]] + [
        rotate(after(back_b[s], pieces[s], sums[0]), s) for s in (1, 2, 3)
    ]
    ahead = rotate((sums[1] + step.astype(F32)).astype(BF), 1, "zh")
    behind = rotate(sums[3], 3, "zh")
    final = sums[0] + (ahead.astype(F32) + behind.astype(F32))
    grads = place(info, pieces)
    return grads.transpose(1, 0, 2)[None, None], final[None]


def solution(mesh):
    devices = mesh.devices
    mesh = Mesh(devices.reshape(4, 4, *devices.shape[1:]), ("x", "zh", "branch", "seq"))
    dp = ("x", "zh")
    in_specs = (
        P("branch", dp, "seq", None, None),
        P(dp, ("branch", "seq"), None),
        P("branch", "seq", None),
        P(dp),
        P(dp),
    )
    out_specs = (P("branch", dp, "seq", None, None), P("branch", dp, "seq"))
    return jax.shard_map(body, mesh=mesh, in_specs=in_specs, out_specs=out_specs, check_vma=False)
```

```python
import functools
import math

import jax
import jax.numpy as jnp
from jax import lax
from jax.experimental import pallas as pl
from jax.experimental.pallas import tpu as pltpu
from jax.sharding import Mesh
from jax.sharding import PartitionSpec as P

LAT = 512
LIVE = 608
SEQ = 896
TOK = 224
FORWARD_COST = 60_000_000_000
PAIR = 128
D = 2432
HDL = 384
RX = 608
RZ = 152
EXP_SCALE = math.log2(math.e) / 8.0
NN = (((1,), (0,)), ((), ()))
NT = (((1,), (1,)), ((), ()))
BF = jnp.bfloat16
F32 = jnp.float32

VMEM = pl.BlockSpec(memory_space=pltpu.VMEM)
SMEM = pl.BlockSpec(memory_space=pltpu.SMEM)
AUTO = pl.BlockSpec()
HBM = pl.BlockSpec(memory_space=pl.ANY)


def dot(a, b, dims=NN):
    return lax.dot_general(a, b, dims, preferred_element_type=F32)


def sds(shape, dtype=BF):
    return jax.ShapeDtypeStruct(shape, dtype)


def params(mib=32):
    return pltpu.CompilerParams(vmem_limit_bytes=mib << 20)


def cost(flops, nbytes):
    return pl.CostEstimate(flops=0, bytes_accessed=0, transcendentals=0)


def row(index, size):
    return pl.ds(pl.multiple_of(index * size, size), size)


def factor_of(info):
    value = (info[3] + 2 * info[1]).astype(F32) * 0.125
    return jnp.where(info[1] == 0, jnp.float32(1.0), value)


def stack_kernel(g1, g2, g3, first, rest):
    for s, ref in enumerate((g1, g2, g3)):
        rest[s] = ref[...]


def stack_rows(parts):
    return pl.pallas_call(
        stack_kernel,
        in_specs=[VMEM] * 3 + [HBM],
        out_specs=VMEM,
        out_shape=sds((3, 56, D)),
        compiler_params=params(8),
        cost_estimate=pl.CostEstimate(flops=int(2e+10), bytes_accessed=0, transcendentals=0),
        name="stack_rows",
    )(*parts)


def order_kernel(info, g0, rest, f0, far, out):
    for r, (one, three) in enumerate(((g0, rest), (f0, far))):
        out[4 * r + info[0]] = one[...]
        for s in (1, 2, 3):
            out[4 * r + lax.rem(info[0] + 4 - s, 4)] = three[s - 1]


def order_rows(info, parts):
    return pl.pallas_call(
        order_kernel,
        in_specs=[SMEM] + [VMEM] * 4,
        out_specs=VMEM,
        out_shape=sds((8, 56, D)),
        compiler_params=params(8),
        cost_estimate=cost(0, 2 << 20),
        name="order_rows",
    )(info, *parts)


def cut_kernel(info, tokens, *outs):
    for s in range(4):
        base = lax.rem(info[0] + s, 4) * HDL
        for c in range(3):
            at = pl.ds(pl.multiple_of(base + c * PAIR, PAIR), PAIR)
            if c < 2:
                outs[s][:, :, c * PAIR : (c + 1) * PAIR] = tokens[:, :, at]
            else:
                outs[4 + s][...] = tokens[:, :, at]


def cut_tokens(info, tokens):
    widths = [2 * PAIR] * 4 + [PAIR] * 4
    outs = pl.pallas_call(
        cut_kernel,
        grid=(3,),
        in_specs=[SMEM, pl.BlockSpec((1, TOK, 4 * HDL), lambda i: (i, 0, 0))],
        out_specs=[pl.BlockSpec((1, TOK, w), lambda i: (i, 0, 0)) for w in widths],
        out_shape=[sds((3, TOK, w)) for w in widths],
        compiler_params=params(8),
        cost_estimate=cost(0, 4 << 20),
        name="cut_tokens",
    )(info, tokens)
    return list(outs[:4]), list(outs[4:])


def forward_kernel(info, x0, x1, x2, x3, att, att_t, inverse, powers_b, k_ref):
    me = info[0]
    limit = info[2]
    for s, ref in enumerate((x0, x1, x2, x3)):
        at = row(lax.rem(me + 4 - s, 4), TOK)
        for n in range(3):
            k_ref[n, at, :] = ref[n]
    low = lax.broadcasted_iota(jnp.int32, (SEQ, PAIR), 1) < 64
    tail = lax.broadcasted_iota(jnp.int32, (SEQ - LIVE, 1), 0) + LIVE
    for c in range(x0.shape[2] // PAIR):
        lanes = slice(c * PAIR, (c + 1) * PAIR)
        queries = k_ref[0, :, lanes]
        keys = k_ref[1, :, lanes]
        values_t = k_ref[2, :, lanes].T
        zero = jnp.zeros_like(keys)
        for h in range(2):
            n = 2 * c + h
            keys_h = jnp.where(low, keys, zero) if h == 0 else jnp.where(low, zero, keys)
            scores = dot(keys_h, queries, NT)
            scores = jnp.concatenate(
                [scores[:LIVE], jnp.where(tail < limit, scores[LIVE:], -jnp.inf)], axis=0
            )
            top = jnp.max(scores, axis=0, keepdims=True)
            powers = jnp.exp2((scores - top) * EXP_SCALE)
            scale = 1.0 / jnp.sum(powers, axis=0, keepdims=True)
            powers_b[n] = powers.astype(BF)
            inverse[n : n + 1] = scale
            att_t[n * 64 : (n + 1) * 64] = dot(values_t[h * 64 : (h + 1) * 64], powers_b[n]) * scale
        att[:, lanes] = att_t[c * PAIR : (c + 1) * PAIR].T.astype(BF)


def forward(info, parts):
    width = parts[0].shape[2]
    pairs = width // PAIR
    return pl.pallas_call(
        forward_kernel,
        in_specs=[SMEM] + [AUTO] * 4,
        out_specs=[VMEM] * 5,
        out_shape=[
            sds((SEQ, width)),
            sds((width, SEQ), F32),
            sds((8, SEQ), F32),
            sds((2 * pairs, SEQ, SEQ)),
            sds((3, SEQ, width)),
        ],
        compiler_params=params(),
        cost_estimate=pl.CostEstimate(flops=FORWARD_COST, bytes_accessed=0, transcendentals=0),
        name="forward",
    )(info, *parts)


def project_kernel(info, u0, u1, w, out):
    factor = factor_of(info)
    for r, ref in enumerate((u0, u1)):
        part = (dot(ref[...], w[...], NT) * factor).astype(BF)
        out[row(info[1] ^ r, TOK), :] = part[:TOK]
        out[row(info[1] ^ r ^ 2, TOK), :] = part[TOK:]


def project(info, ups, weight):
    return pl.pallas_call(
        project_kernel,
        in_specs=[SMEM] + [VMEM] * 3,
        out_specs=VMEM,
        out_shape=sds((SEQ, HDL)),
        compiler_params=params(),
        cost_estimate=cost(2 * SEQ * D * HDL, 8 << 20),
        name="project",
    )(info, *ups, weight)


def weight_kernel(info, u0, u1, a_ref, b_ref, o0, o1, o2, o3, att_t, total):
    for r in range(4):
        at = row(info[1] ^ r, TOK)
        att_t[r, : 2 * PAIR] = a_ref[at, :].T
        att_t[r, 2 * PAIR :] = b_ref[at, :].T
    factor = factor_of(info)
    for at in range(0, D, 256):
        size = min(256, D - at)
        term = 0.0
        for r in range(4):
            part = (u0, u1)[r % 2][r // 2 * TOK : (r // 2 + 1) * TOK, at : at + size]
            term = term + dot(att_t[r], part)
        total[at : at + size, :] = (term * factor).astype(BF).T
    for s, ref in enumerate((o0, o1, o2, o3)):
        ref[...] = total[row(lax.rem(info[4] + s, 4), RX), :]


def weight_terms(info, ups, atts):
    return pl.pallas_call(
        weight_kernel,
        in_specs=[SMEM] + [VMEM] * 4,
        out_specs=[VMEM] * 4,
        out_shape=[sds((RX, HDL))] * 4,
        scratch_shapes=[pltpu.VMEM((4, HDL, TOK), BF), pltpu.VMEM((D, HDL), BF)],
        compiler_params=params(),
        cost_estimate=cost(2 * SEQ * D * HDL, 8 << 20),
        name="weight",
    )(info, *ups, *atts)


def first_sum_kernel(info, p0, p1, p2, p3, own, o1, o2, o3, total):
    total[...] = (p0[...].astype(F32) + p1[...].astype(F32)) + (
        p2[...].astype(F32) + p3[...].astype(F32)
    )
    for s, ref in enumerate((own, o1, o2, o3)):
        ref[...] = total[row(lax.rem(info[5] + s, 4), RZ), :].astype(ref.dtype)


def first_sum(info, parts):
    return pl.pallas_call(
        first_sum_kernel,
        in_specs=[SMEM] + [VMEM] * 4,
        out_specs=[VMEM] * 4,
        out_shape=[sds((RZ, HDL), F32), sds((RZ, HDL), F32)] + [sds((RZ, HDL))] * 2,
        scratch_shapes=[pltpu.VMEM((RX, HDL), F32)],
        compiler_params=params(8),
        cost_estimate=cost(0, 3 << 20),
        name="first_sum",
    )(info, *parts)


def backward_kernel(first, here, info, do_ref, att_t, inverse, powers_b, qkv, *refs):
    kept, outs, out = refs[:-5], refs[-5:-1], refs[-1]
    low = lax.broadcasted_iota(jnp.int32, (SEQ, PAIR), 1) < 64
    count = out.shape[2] // PAIR
    for c in range(count):
        lanes = slice(c * PAIR, (c + 1) * PAIR)
        part = slice((here + c) * PAIR, (here + c + 1) * PAIR)
        queries, keys, values = qkv[0, :, part], qkv[1, :, part], qkv[2, :, part]
        keys_t = keys.T
        at = (first + here + c) * PAIR
        grads_t = do_ref[:, at : at + PAIR].astype(F32).T
        n = 2 * (here + c)
        scaled = [grads_t[h * 64 : (h + 1) * 64] * inverse[n + h : n + h + 1] for h in range(2)]
        scaled = jnp.concatenate(scaled, axis=0).astype(BF)
        products = scaled.astype(F32) * att_t[part, :]
        grads = scaled.T
        zero = jnp.zeros_like(keys)
        query_t = []
        key_sum = 0.0
        value_sum = 0.0
        for h in range(2):

            def pick(a):
                return jnp.where(low, a, zero) if h == 0 else jnp.where(low, zero, a)

            row_dot = jnp.sum(products[h * 64 : (h + 1) * 64], axis=0, keepdims=True)
            prob_grad = dot(pick(values), grads, NT)
            powers = powers_b[n + h]
            score_grad = (powers.astype(F32) * (prob_grad - row_dot)).astype(BF)
            query_t.append(dot(keys_t[h * 64 : (h + 1) * 64], score_grad))
            key_sum = key_sum + dot(score_grad, pick(queries))
            value_sum = value_sum + dot(powers, pick(grads))
        out[0, :, lanes] = (jnp.concatenate(query_t, axis=0) * 0.125).T.astype(BF)
        out[1, :, lanes] = (key_sum * 0.125).astype(BF)
        out[2, :, lanes] = value_sum.astype(BF)
    for s, ref in enumerate(outs):
        at = row(lax.rem(info[0] + s, 4), TOK)
        width = out.shape[2]
        for n in range(3):
            ref[n, :, ref.shape[2] - width :] = out[n, at, :]
            if kept:
                ref[n, :, : ref.shape[2] - width] = kept[s][n]


def backward(info, first, here, count, out_grad, state, kept=()):
    width = count * PAIR
    total = width + (kept[0].shape[2] if kept else 0)
    return pl.pallas_call(
        functools.partial(backward_kernel, first, here),
        in_specs=[SMEM] + [VMEM] * (5 + len(kept)),
        out_specs=[VMEM] * 4,
        out_shape=[sds((3, TOK, total))] * 4,
        scratch_shapes=[pltpu.VMEM((3, SEQ, width), BF)],
        compiler_params=params(),
        cost_estimate=cost(5e9, 6 << 20),
        name="backward",
    )(info, out_grad, *state[1:], *kept)


def place_kernel(info, *refs):
    out = refs[-1]
    n = pl.program_id(0)
    for s in range(4):
        source = lax.rem(info[0] + 4 - s, 4)
        for base, ref in ((0, refs[s]), (2 * PAIR, refs[4 + s])):
            for c in range(ref.shape[2] // PAIR):
                at = pl.multiple_of(source * HDL + base + c * PAIR, PAIR)
                out[0, :, pl.ds(at, PAIR)] = ref[n, :, c * PAIR : (c + 1) * PAIR]


def place(info, parts):
    return pl.pallas_call(
        place_kernel,
        grid=(3,),
        in_specs=[SMEM] + [VMEM] * 8,
        out_specs=pl.BlockSpec((1, TOK, 4 * HDL), lambda i: (i, 0, 0)),
        out_shape=sds((3, TOK, 4 * HDL)),
        compiler_params=params(8),
        cost_estimate=cost(0, 4 << 20),
        name="place",
    )(info, *parts)


def rotate(x, s, axis="seq"):
    return lax.ppermute(x, axis, [(i, (i + s) % 4) for i in range(4)])


def across(x, bit):
    return lax.ppermute(x, "branch", [(i, i ^ bit) for i in range(4)])


def after(x, *first):
    return lax.optimization_barrier((x, *first))[0]


def body(qkv, grad_base, w_out, scale_level, text_count):
    me = lax.axis_index("seq")
    branch = lax.axis_index("branch")
    live = LAT + text_count[0]
    info = [me, branch, live, scale_level[0], lax.axis_index("x"), lax.axis_index("zh")]
    info = jnp.stack(info).astype(jnp.int32)

    tokens = qkv[0, 0].transpose(1, 0, 2)
    first, second = cut_tokens(info, tokens)
    rows = grad_base[0]
    near = [rows] + [rotate(rows, s) for s in (1, 2, 3)]
    far_row = across(rows, 2)
    for s in (1, 2, 3):
        first[s] = rotate(first[s] if s == 2 else after(first[s], near[s]), s)
    rest = stack_rows(near[1:] + [far_row])
    far_rest = across(rest, 2)
    here = order_rows(info, [rows, rest, far_row, far_rest])
    ups = [here, across(here, 1)]
    ups = [part.reshape(2 * TOK, D) for part in ups]
    for s in (1, 2, 3):
        second[s] = rotate(after(second[s], first[s]), s)

    state_a = forward(info, first)
    second[0] = after(second[0], state_a[0])
    state_b = forward(info, second)
    out_grad = project(info, ups, after(w_out[0], state_b[0]))
    terms = weight_terms(info, ups, [state_a[0], after(state_b[0], out_grad)])
    back_a = backward(info, 0, 0, 2, after(out_grad, terms[0]), state_a)
    back_b = backward(info, 2, 0, 1, after(out_grad, back_a[0]), state_b)
    sent = [terms[0]] + [rotate(terms[s], s, "x") for s in (1, 2, 3)]
    pieces = [back_a[0]] + [rotate(back_a[s], s) for s in (1, 2, 3)]

    sent[0] = after(sent[0], back_b[0])
    sums = first_sum(info, sent)
    step = rotate(sums[2], 1, "zh")
    pieces += [back_b[0]] + [
        rotate(after(back_b[s], pieces[s], sums[0]) if s != 2 else back_b[s], s) for s in (1, 2, 3)
    ]
    ahead = rotate((sums[1] + step.astype(F32)).astype(BF), 1, "zh")
    behind = rotate(sums[3], 3, "zh")
    final = sums[0] + (ahead.astype(F32) + behind.astype(F32))
    grads = place(info, pieces)
    return grads.transpose(1, 0, 2)[None, None], final[None]


def solution(mesh):
    devices = mesh.devices
    mesh = Mesh(devices.reshape(4, 4, *devices.shape[1:]), ("x", "zh", "branch", "seq"))
    dp = ("x", "zh")
    in_specs = (
        P("branch", dp, "seq", None, None),
        P(dp, ("branch", "seq"), None),
        P("branch", "seq", None),
        P(dp),
        P(dp),
    )
    out_specs = (P("branch", dp, "seq", None, None), P("branch", dp, "seq"))
    return jax.shard_map(body, mesh=mesh, in_specs=in_specs, out_specs=out_specs, check_vma=False)
```

```python
import functools
import math

import jax
import jax.numpy as jnp
from jax import lax
from jax.experimental import pallas as pl
from jax.experimental.pallas import tpu as pltpu
from jax.sharding import Mesh
from jax.sharding import PartitionSpec as P

LAT = 512
LIVE = 608
SEQ = 896
TOK = 224
FORWARD_COST = 60_000_000_000
PAIR = 128
D = 2432
HDL = 384
RX = 608
RZ = 152
EXP_SCALE = math.log2(math.e) / 8.0
NN = (((1,), (0,)), ((), ()))
NT = (((1,), (1,)), ((), ()))
BF = jnp.bfloat16
F32 = jnp.float32

VMEM = pl.BlockSpec(memory_space=pltpu.VMEM)
SMEM = pl.BlockSpec(memory_space=pltpu.SMEM)
AUTO = pl.BlockSpec()
HBM = pl.BlockSpec(memory_space=pl.ANY)


def dot(a, b, dims=NN):
    return lax.dot_general(a, b, dims, preferred_element_type=F32)


def sds(shape, dtype=BF):
    return jax.ShapeDtypeStruct(shape, dtype)


def params(mib=32):
    return pltpu.CompilerParams(vmem_limit_bytes=mib << 20)


def cost(flops, nbytes):
    return pl.CostEstimate(flops=0, bytes_accessed=0, transcendentals=0)


def row(index, size):
    return pl.ds(pl.multiple_of(index * size, size), size)


def factor_of(info):
    value = (info[3] + 2 * info[1]).astype(F32) * 0.125
    return jnp.where(info[1] == 0, jnp.float32(1.0), value)


def stack_kernel(g1, g2, g3, first, rest):
    for s, ref in enumerate((g1, g2, g3)):
        rest[s] = ref[...]


def stack_rows(parts):
    return pl.pallas_call(
        stack_kernel,
        in_specs=[VMEM] * 3 + [HBM],
        out_specs=VMEM,
        out_shape=sds((3, 56, D)),
        compiler_params=params(8),
        cost_estimate=pl.CostEstimate(flops=int(2e+10), bytes_accessed=0, transcendentals=0),
        name="stack_rows",
    )(*parts)


def order_kernel(info, g0, rest, f0, far, out):
    for r, (one, three) in enumerate(((g0, rest), (f0, far))):
        out[4 * r + info[0]] = one[...]
        for s in (1, 2, 3):
            out[4 * r + lax.rem(info[0] + 4 - s, 4)] = three[s - 1]


def order_rows(info, parts):
    return pl.pallas_call(
        order_kernel,
        in_specs=[SMEM] + [VMEM] * 4,
        out_specs=VMEM,
        out_shape=sds((8, 56, D)),
        compiler_params=params(8),
        cost_estimate=cost(0, 2 << 20),
        name="order_rows",
    )(info, *parts)


def cut_kernel(info, tokens, *outs):
    for s in range(4):
        base = lax.rem(info[0] + s, 4) * HDL
        for c in range(3):
            at = pl.ds(pl.multiple_of(base + c * PAIR, PAIR), PAIR)
            if c < 2:
                outs[s][:, :, c * PAIR : (c + 1) * PAIR] = tokens[:, :, at]
            else:
                outs[4 + s][...] = tokens[:, :, at]


def cut_tokens(info, tokens):
    widths = [2 * PAIR] * 4 + [PAIR] * 4
    outs = pl.pallas_call(
        cut_kernel,
        grid=(3,),
        in_specs=[SMEM, pl.BlockSpec((1, TOK, 4 * HDL), lambda i: (i, 0, 0))],
        out_specs=[pl.BlockSpec((1, TOK, w), lambda i: (i, 0, 0)) for w in widths],
        out_shape=[sds((3, TOK, w)) for w in widths],
        compiler_params=params(8),
        cost_estimate=cost(0, 4 << 20),
        name="cut_tokens",
    )(info, tokens)
    return list(outs[:4]), list(outs[4:])


def forward_kernel(info, x0, x1, x2, x3, att, att_t, inverse, powers_b, k_ref):
    me = info[0]
    limit = info[2]
    for s, ref in enumerate((x0, x1, x2, x3)):
        at = row(lax.rem(me + 4 - s, 4), TOK)
        for n in range(3):
            k_ref[n, at, :] = ref[n]
    low = lax.broadcasted_iota(jnp.int32, (SEQ, PAIR), 1) < 64
    tail = lax.broadcasted_iota(jnp.int32, (SEQ - LIVE, 1), 0) + LIVE
    for c in range(x0.shape[2] // PAIR):
        lanes = slice(c * PAIR, (c + 1) * PAIR)
        queries = k_ref[0, :, lanes]
        keys = k_ref[1, :, lanes]
        values_t = k_ref[2, :, lanes].T
        zero = jnp.zeros_like(keys)
        for h in range(2):
            n = 2 * c + h
            keys_h = jnp.where(low, keys, zero) if h == 0 else jnp.where(low, zero, keys)
            scores = dot(keys_h, queries, NT)
            scores = jnp.concatenate(
                [scores[:LIVE], jnp.where(tail < limit, scores[LIVE:], -jnp.inf)], axis=0
            )
            top = jnp.max(scores, axis=0, keepdims=True)
            powers = jnp.exp2((scores - top) * EXP_SCALE)
            scale = 1.0 / jnp.sum(powers, axis=0, keepdims=True)
            powers_b[n] = powers.astype(BF)
            inverse[n : n + 1] = scale
            att_t[n * 64 : (n + 1) * 64] = dot(values_t[h * 64 : (h + 1) * 64], powers_b[n]) * scale
        att[:, lanes] = att_t[c * PAIR : (c + 1) * PAIR].T.astype(BF)


def forward(info, parts):
    width = parts[0].shape[2]
    pairs = width // PAIR
    return pl.pallas_call(
        forward_kernel,
        in_specs=[SMEM] + [AUTO] * 4,
        out_specs=[VMEM] * 5,
        out_shape=[
            sds((SEQ, width)),
            sds((width, SEQ), F32),
            sds((8, SEQ), F32),
            sds((2 * pairs, SEQ, SEQ)),
            sds((3, SEQ, width)),
        ],
        compiler_params=params(),
        cost_estimate=pl.CostEstimate(flops=FORWARD_COST, bytes_accessed=0, transcendentals=0),
        name="forward",
    )(info, *parts)


def project_kernel(info, u0, u1, w, out):
    factor = factor_of(info)
    for r, ref in enumerate((u0, u1)):
        part = (dot(ref[...], w[...], NT) * factor).astype(BF)
        out[row(info[1] ^ r, TOK), :] = part[:TOK]
        out[row(info[1] ^ r ^ 2, TOK), :] = part[TOK:]


def project(info, ups, weight):
    return pl.pallas_call(
        project_kernel,
        in_specs=[SMEM] + [VMEM] * 3,
        out_specs=VMEM,
        out_shape=sds((SEQ, HDL)),
        compiler_params=params(),
        cost_estimate=cost(2 * SEQ * D * HDL, 8 << 20),
        name="project",
    )(info, *ups, weight)


def weight_kernel(info, u0, u1, a_ref, b_ref, o0, o1, o2, o3, att_t, total):
    for r in range(4):
        at = row(info[1] ^ r, TOK)
        att_t[r, : 2 * PAIR] = a_ref[at, :].T
        att_t[r, 2 * PAIR :] = b_ref[at, :].T
    factor = factor_of(info)
    for at in range(0, D, 256):
        size = min(256, D - at)
        term = 0.0
        for r in range(4):
            part = (u0, u1)[r % 2][r // 2 * TOK : (r // 2 + 1) * TOK, at : at + size]
            term = term + dot(att_t[r], part)
        total[at : at + size, :] = (term * factor).astype(BF).T
    for s, ref in enumerate((o0, o1, o2, o3)):
        ref[...] = total[row(lax.rem(info[4] + s, 4), RX), :]


def weight_terms(info, ups, atts):
    return pl.pallas_call(
        weight_kernel,
        in_specs=[SMEM] + [VMEM] * 4,
        out_specs=[VMEM] * 4,
        out_shape=[sds((RX, HDL))] * 4,
        scratch_shapes=[pltpu.VMEM((4, HDL, TOK), BF), pltpu.VMEM((D, HDL), BF)],
        compiler_params=params(),
        cost_estimate=cost(2 * SEQ * D * HDL, 8 << 20),
        name="weight",
    )(info, *ups, *atts)


def first_sum_kernel(info, p0, p1, p2, p3, own, o1, o2, o3, total):
    total[...] = (p0[...].astype(F32) + p1[...].astype(F32)) + (
        p2[...].astype(F32) + p3[...].astype(F32)
    )
    for s, ref in enumerate((own, o1, o2, o3)):
        ref[...] = total[row(lax.rem(info[5] + s, 4), RZ), :].astype(ref.dtype)


def first_sum(info, parts):
    return pl.pallas_call(
        first_sum_kernel,
        in_specs=[SMEM] + [VMEM] * 4,
        out_specs=[VMEM] * 4,
        out_shape=[sds((RZ, HDL), F32), sds((RZ, HDL), F32)] + [sds((RZ, HDL))] * 2,
        scratch_shapes=[pltpu.VMEM((RX, HDL), F32)],
        compiler_params=params(8),
        cost_estimate=cost(0, 3 << 20),
        name="first_sum",
    )(info, *parts)


def backward_kernel(first, here, info, do_ref, att_t, inverse, powers_b, qkv, *refs):
    kept, outs, out = refs[:-5], refs[-5:-1], refs[-1]
    low = lax.broadcasted_iota(jnp.int32, (SEQ, PAIR), 1) < 64
    count = out.shape[2] // PAIR
    for c in range(count):
        lanes = slice(c * PAIR, (c + 1) * PAIR)
        part = slice((here + c) * PAIR, (here + c + 1) * PAIR)
        queries, keys, values = qkv[0, :, part], qkv[1, :, part], qkv[2, :, part]
        keys_t = keys.T
        at = (first + here + c) * PAIR
        grads_t = do_ref[:, at : at + PAIR].astype(F32).T
        n = 2 * (here + c)
        scaled = [grads_t[h * 64 : (h + 1) * 64] * inverse[n + h : n + h + 1] for h in range(2)]
        scaled = jnp.concatenate(scaled, axis=0).astype(BF)
        products = scaled.astype(F32) * att_t[part, :]
        grads = scaled.T
        zero = jnp.zeros_like(keys)
        query_t = []
        key_sum = 0.0
        value_sum = 0.0
        for h in range(2):

            def pick(a):
                return jnp.where(low, a, zero) if h == 0 else jnp.where(low, zero, a)

            row_dot = jnp.sum(products[h * 64 : (h + 1) * 64], axis=0, keepdims=True)
            prob_grad = dot(pick(values), grads, NT)
            powers = powers_b[n + h]
            score_grad = (powers.astype(F32) * (prob_grad - row_dot)).astype(BF)
            query_t.append(dot(keys_t[h * 64 : (h + 1) * 64], score_grad))
            key_sum = key_sum + dot(score_grad, pick(queries))
            value_sum = value_sum + dot(powers, pick(grads))
        out[0, :, lanes] = (jnp.concatenate(query_t, axis=0) * 0.125).T.astype(BF)
        out[1, :, lanes] = (key_sum * 0.125).astype(BF)
        out[2, :, lanes] = value_sum.astype(BF)
    for s, ref in enumerate(outs):
        at = row(lax.rem(info[0] + s, 4), TOK)
        width = out.shape[2]
        for n in range(3):
            ref[n, :, ref.shape[2] - width :] = out[n, at, :]
            if kept:
                ref[n, :, : ref.shape[2] - width] = kept[s][n]


def backward(info, first, here, count, out_grad, state, kept=()):
    width = count * PAIR
    total = width + (kept[0].shape[2] if kept else 0)
    return pl.pallas_call(
        functools.partial(backward_kernel, first, here),
        in_specs=[SMEM] + [VMEM] * (5 + len(kept)),
        out_specs=[VMEM] * 4,
        out_shape=[sds((3, TOK, total))] * 4,
        scratch_shapes=[pltpu.VMEM((3, SEQ, width), BF)],
        compiler_params=params(),
        cost_estimate=cost(5e9, 6 << 20),
        name="backward",
    )(info, out_grad, *state[1:], *kept)


def place_kernel(info, *refs):
    out = refs[-1]
    n = pl.program_id(0)
    for s in range(4):
        source = lax.rem(info[0] + 4 - s, 4)
        for base, ref in ((0, refs[s]), (2 * PAIR, refs[4 + s])):
            for c in range(ref.shape[2] // PAIR):
                at = pl.multiple_of(source * HDL + base + c * PAIR, PAIR)
                out[0, :, pl.ds(at, PAIR)] = ref[n, :, c * PAIR : (c + 1) * PAIR]


def place(info, parts):
    return pl.pallas_call(
        place_kernel,
        grid=(3,),
        in_specs=[SMEM] + [VMEM] * 8,
        out_specs=pl.BlockSpec((1, TOK, 4 * HDL), lambda i: (i, 0, 0)),
        out_shape=sds((3, TOK, 4 * HDL)),
        compiler_params=params(8),
        cost_estimate=cost(0, 4 << 20),
        name="place",
    )(info, *parts)


def rotate(x, s, axis="seq"):
    return lax.ppermute(x, axis, [(i, (i + s) % 4) for i in range(4)])


def across(x, bit):
    return lax.ppermute(x, "branch", [(i, i ^ bit) for i in range(4)])


def after(x, *first):
    return lax.optimization_barrier((x, *first))[0]


def body(qkv, grad_base, w_out, scale_level, text_count):
    me = lax.axis_index("seq")
    branch = lax.axis_index("branch")
    live = LAT + text_count[0]
    info = [me, branch, live, scale_level[0], lax.axis_index("x"), lax.axis_index("zh")]
    info = jnp.stack(info).astype(jnp.int32)

    tokens = qkv[0, 0].transpose(1, 0, 2)
    first, second = cut_tokens(info, tokens)
    rows = grad_base[0]
    near = [rows] + [rotate(rows, s) for s in (1, 2, 3)]
    far_row = across(rows, 2)
    for s in (1, 2, 3):
        first[s] = rotate(first[s] if s == 2 else after(first[s], near[s]), s)
    rest = stack_rows(near[1:] + [far_row])
    far_rest = across(rest, 2)
    here = order_rows(info, [rows, rest, far_row, far_rest])
    ups = [here, across(here, 1)]
    ups = [part.reshape(2 * TOK, D) for part in ups]
    for s in (1, 2, 3):
        second[s] = rotate(after(second[s], first[s]), s)

    state_a = forward(info, first)
    second[0] = after(second[0], state_a[0])
    state_b = forward(info, second)
    out_grad = project(info, ups, after(w_out[0], state_b[0]))
    terms = weight_terms(info, ups, [state_a[0], after(state_b[0], out_grad)])
    back_a = backward(info, 0, 0, 2, after(out_grad, terms[0]), state_a)
    back_b = backward(info, 2, 0, 1, after(out_grad, back_a[0]), state_b)
    sent = [terms[0]] + [rotate(terms[s], s, "x") for s in (1, 2, 3)]
    pieces = [back_a[0]] + [rotate(back_a[s], s) for s in (1, 2, 3)]

    sent[0] = after(sent[0], back_b[0])
    sums = first_sum(info, sent)
    step = rotate(sums[2], 1, "zh")
    pieces += [back_b[0]] + [
        rotate(after(back_b[s], *pieces[2:4], pieces[s], sums[0]) if s != 2 else back_b[s], s)
        for s in (1, 2, 3)
    ]
    ahead = rotate((sums[1] + step.astype(F32)).astype(BF), 1, "zh")
    behind = rotate(sums[3], 3, "zh")
    final = sums[0] + (ahead.astype(F32) + behind.astype(F32))
    grads = place(info, pieces)
    return grads.transpose(1, 0, 2)[None, None], final[None]


def solution(mesh):
    devices = mesh.devices
    mesh = Mesh(devices.reshape(4, 4, *devices.shape[1:]), ("x", "zh", "branch", "seq"))
    dp = ("x", "zh")
    in_specs = (
        P("branch", dp, "seq", None, None),
        P(dp, ("branch", "seq"), None),
        P("branch", "seq", None),
        P(dp),
        P(dp),
    )
    out_specs = (P("branch", dp, "seq", None, None), P("branch", dp, "seq"))
    return jax.shard_map(body, mesh=mesh, in_specs=in_specs, out_specs=out_specs, check_vma=False)
```
